512 devices in a mesh: section: 32 (over y, x, core), expert: 16 (over z).
Axes of the slice: x: 4, y: 4, z: 16, core: 2. Of those that a mesh axis runs over, the one named last changes fastest.
Arguments:
- inputs_down: bfloat16 [32, 1024, 3584], P('section', 'expert'), may hold values from -6 to 6
- inputs_up: bfloat16 [32, 1024, 3584], P('section', 'expert'), may hold values from -6 to 6
- routes_down: int32 [32, 1024, 1], P('section', 'expert'), may hold values from 0 to 1; in each aligned block of 64 rows (0 to 63, 64 to 127, ..., all dimensions but the last counted through in order) at most 34 rows name the same one
- routes_up: int32 [32, 1024, 1], P('section', 'expert'), may hold values from 0 to 1; in each aligned block of 64 rows (0 to 63, 64 to 127, ..., all dimensions but the last counted through in order) at most 34 rows name the same one
- probs_down: float32 [32, 1024, 1], P('section', 'expert'), may hold values from 0.5 to 1.5
- probs_up: float32 [32, 1024, 1], P('section', 'expert'), may hold values from 0.5 to 1.5
- norm_gain: float32 [32, 3584], P('section'), may hold values from 0.1 to 1.9
- gate_weight: bfloat16 [32, 3584, 2048], P('section', None, 'expert'), may hold values from -0.09375 to 0.09375
- up_weight: bfloat16 [32, 3584, 2048], P('section', None, 'expert'), may hold values from -0.09375 to 0.09375
- down_weight: bfloat16 [32, 2048, 3584], P('section', 'expert'), may hold values from -0.1875 to 0.1875
Outputs:
- outputs_down: bfloat16 [32, 1024, 3584], P('section', 'expert')
- outputs_up: bfloat16 [32, 1024, 3584], P('section', 'expert')
The draws below stay inside these ranges and needn't reach their ends.
Inputs may be any that keep to these rules, and one draw needn't show every extreme that they name: `routes_down`: among the tokens of one device, each expert is named by at most 34 tokens, a bound that some block reaches. `routes_up`: among the tokens of one device, each expert is named by at most 34 tokens, a bound that some block reaches.
All inputs are finite; a program needn't handle non-finite values.
Results may differ from the reference program's by a relative error of at most 0.0053.
Values may be sent and summed in bfloat16 or wider, within the bound.
No kernel may reach another device: no remote copies, remote signals or barrier semaphores. Data moves between devices by JAX's collectives and lax.ppermute only.
A program may use at most 128 MiB of HBM per device.

```python
import math
import jax
import jax.numpy as jnp
import numpy as np
from jax import lax

D = 3584
HID = 1024
EXP_SECTION = 2
TOPK = 1
ROWS = 64
CAP = 34
TOK = 1024
N_SECTION = 32
N_EXPERT = 16


def block_levels(key, shape, split, smallest, largest):
    loudness = 1.0
    for dim, shards_of in split:
        draws = jax.random.uniform(jax.random.fold_in(jax.random.fold_in(key, 6), dim), (shards_of,), jnp.float32, smallest / len(split), largest / len(split))
        loudness = loudness * jnp.repeat(jnp.exp(draws), shape[dim] // shards_of).reshape((-1,) + (1,) * (len(shape) - 1 - dim))
    return loudness


def routed_block(rng, own, number, rows, count, top, limit, lean):
    sequence = jax.random.permutation(rng, count)
    crowded, usual = portions_of(count, rows * top, limit, lean, True), portions_of(count, rows * top, limit, lean, False)
    places = jnp.arange(count)

    def named(tallies, offset_by):
        used = int((tallies > 0).sum())
        fixed = max(1, used // 4)
        passed = fixed + (places - fixed + offset_by * (used - fixed)) % max(1, count - fixed)
        return jnp.zeros((count,), jnp.int32).at[sequence[jnp.where(places < fixed, places, passed)]].set(jnp.asarray(tallies, jnp.int32))

    tallies = jnp.where(number % 4 == 0, named(crowded, number // 4), named(usual, number - number // 4 - 1))
    mixed = jax.random.permutation(jax.random.fold_in(own, 3), count)
    giver, receiver = mixed[0:count // 2 * 2:2], mixed[1:count // 2 * 2:2]
    room = jnp.minimum(tallies[giver] - 1, limit - tallies[receiver]) // 2
    room = jnp.where((giver == sequence[0]) | (receiver == sequence[0]) | (tallies[receiver] == 0), 0, jnp.maximum(room, 0))
    passed = jax.random.randint(jax.random.fold_in(own, 4), (count // 2,), 0, 1 << 20) % (room + 1)
    tallies = tallies.at[giver].add(-passed).at[receiver].add(passed)
    members = jnp.searchsorted(jnp.cumsum(tallies), jnp.arange(rows * top), side="right").astype(jnp.int32)
    listing = members.reshape(top, rows).T
    listing = listing[jax.random.permutation(jax.random.fold_in(own, 1), rows)]
    offset_by = jax.random.randint(jax.random.fold_in(own, 2), (rows, 1), 0, top)
    return jnp.take_along_axis(listing, (jnp.arange(top)[None, :] + offset_by) % top, axis=1)


def portions_of(amount, total, most, skew, full):
    weights = [(1 << 20) // math.isqrt(grade ** skew) + 1 for grade in range(1, amount + 1)]
    largest = most if full else min(most, max(-(-total // amount), total * weights[0] // sum(weights)))
    least = 1 if total - largest >= amount - 1 else 0
    given, rest = [largest] + [least] * (amount - 1), total - largest - least * (amount - 1)
    while rest > 0:
        free = [i for i in range(1, amount) if given[i] < largest] or [i for i in range(1, amount) if given[i] < most]
        mass, left = sum([weights[i] for i in free]), rest
        for i in free:
            more = min(most - given[i], max(1, left * weights[i] // mass), rest)
            given[i] = given[i] + more
            rest = rest - more
    return np.array(given)


def normal_values(key, dims, scale, limit, cuts=(), held_as=jnp.bfloat16):
    result = jax.random.normal(key, dims, jnp.float32) * scale
    if len(cuts) > 0:
        result = block_levels(key, dims, cuts, -0.22, 0.18) * result
    return jnp.clip(result, min=-limit, max=limit).astype(held_as)


def setup_inputs(seed: int = 0) -> dict:
    key_of = jax.random.split(jax.random.key(seed), 11)
    inputs_down = normal_values(key_of[0], (N_SECTION, TOK, D), 1.0, 6.0, ((0, 32), (1, 16)))
    inputs_up = normal_values(key_of[1], (N_SECTION, TOK, D), 1.0, 6.0, ((0, 32), (1, 16)))
    routes_down_keys = jax.random.split(jax.random.fold_in(key_of[2], 1), N_SECTION * TOK // ROWS)
    routes_down_turns = jax.random.permutation(jax.random.fold_in(key_of[2], 3), N_SECTION * TOK // ROWS)
    routes_down = jax.vmap(lambda own, number: routed_block(jax.random.fold_in(key_of[2], 2), own, number, ROWS, EXP_SECTION, TOPK, CAP, 2))(routes_down_keys, routes_down_turns).reshape((N_SECTION, TOK, TOPK))
    routes_up_keys = jax.random.split(jax.random.fold_in(key_of[3], 1), N_SECTION * TOK // ROWS)
    routes_up_turns = jax.random.permutation(jax.random.fold_in(key_of[3], 3), N_SECTION * TOK // ROWS)
    routes_up = jax.vmap(lambda own, number: routed_block(jax.random.fold_in(key_of[3], 2), own, number, ROWS, EXP_SECTION, TOPK, CAP, 2))(routes_up_keys, routes_up_turns).reshape((N_SECTION, TOK, TOPK))
    probs_down = jnp.clip(0.5 + 1.0 * jax.random.uniform(key_of[4], (N_SECTION, TOK, TOPK), jnp.float32) ** block_levels(key_of[4], (N_SECTION, TOK, TOPK), ((0, 32), (1, 16)), -0.2, 0.2), 0.5, 1.5)
    probs_up = jnp.clip(0.5 + 1.0 * jax.random.uniform(key_of[5], (N_SECTION, TOK, TOPK), jnp.float32) ** block_levels(key_of[5], (N_SECTION, TOK, TOPK), ((0, 32), (1, 16)), -0.2, 0.2), 0.5, 1.5)
    norm_gain = jnp.clip(1.0 + 0.18 * jax.random.normal(key_of[6], (N_SECTION, D), jnp.float32), 0.1, 1.9)
    gate_weight = normal_values(key_of[7], (N_SECTION, D, EXP_SECTION * HID), D ** -0.5, 0.09375, ((0, 32), (2, 16)))
    up_weight = normal_values(key_of[8], (N_SECTION, D, EXP_SECTION * HID), D ** -0.5, 0.09375, ((0, 32), (2, 16)))
    down_weight = normal_values(key_of[9], (N_SECTION, EXP_SECTION * HID, D), HID ** -0.5, 0.1875, ((0, 32), (1, 16)))
    return {"inputs_down": inputs_down, "inputs_up": inputs_up, "routes_down": routes_down, "routes_up": routes_up, "probs_down": probs_down, "probs_up": probs_up, "norm_gain": norm_gain, "gate_weight": gate_weight, "up_weight": up_weight, "down_weight": down_weight}


def norm_rows(inputs, gain):
    values = inputs.astype(jnp.float32)
    meansq = lax.optimization_barrier(jnp.mean(values * values, axis=-1, keepdims=True)) + 1e-06
    return (values * lax.rsqrt(meansq) * gain[None, :]).astype(jnp.bfloat16)

def section_layer(inputs, picks, weights_in, gain, gate_weight, up_weight, down_weight):
    shards = N_EXPERT // EXP_SECTION
    hid_dev = HID // shards
    normed = norm_rows(inputs, gain)
    total = jnp.zeros((inputs.shape[0], D), jnp.float32)
    for expert_id in range(EXP_SECTION):
        low = expert_id * HID
        gate = jnp.dot(normed, gate_weight[:, low:low + HID], preferred_element_type=jnp.float32)
        upper = jnp.dot(normed, up_weight[:, low:low + HID], preferred_element_type=jnp.float32)
        hidden = (jax.nn.silu(gate) * upper).astype(jnp.bfloat16)
        hidden = hidden.reshape(inputs.shape[0], shards, hid_dev).astype(jnp.float32)
        downs = down_weight[low:low + HID].reshape(shards, hid_dev, D).astype(jnp.float32)
        parts = jnp.einsum('tkh,khd->tkd', hidden, downs).astype(jnp.bfloat16)
        parts = lax.optimization_barrier(parts).astype(jnp.float32)
        contrib = lax.optimization_barrier(jnp.sum(parts, axis=1))
        chosen = picks[:, 0] == expert_id
        total = total + jnp.where(chosen[:, None], contrib, jnp.float32(0.0))
    moved = inputs.astype(jnp.float32) + weights_in[:, 0:1] * total
    return moved.astype(jnp.bfloat16)

def run_direction(inputs, picks, weights_in, norm_gain, gate_weight, up_weight, down_weight):

    def one_section(items):
        return section_layer(*items)
    return lax.map(one_section, (inputs, picks, weights_in, norm_gain, gate_weight, up_weight, down_weight))

def reference(inputs_down, inputs_up, routes_down, routes_up, probs_down, probs_up, norm_gain, gate_weight, up_weight, down_weight):
    moved_down = run_direction(inputs_down, routes_down, probs_down, norm_gain, gate_weight, up_weight, down_weight)
    moved_up = run_direction(inputs_up, routes_up, probs_up, norm_gain, gate_weight, up_weight, down_weight)
    return (jnp.roll(moved_down, 1, axis=0), jnp.roll(moved_up, -1, axis=0))
```

```python
import jax
import jax.numpy as jnp
from jax import lax
from jax.experimental import pallas as pl
from jax.experimental.pallas import tpu as pltpu
from jax.sharding import PartitionSpec as P

EXP_SECTION = 2
TAIL = 128
VMEM_LIMIT = 48 * 1024 * 1024


def call(kernel, out_shape, flops, moved, **options):
    return pl.pallas_call(
        kernel,
        out_shape=out_shape,
        cost_estimate=pl.CostEstimate(flops=flops, bytes_accessed=moved, transcendentals=0),
        compiler_params=pltpu.CompilerParams(vmem_limit_bytes=VMEM_LIMIT),
        **options,
    )


def norm_rows(inputs, gain, tail=None):
    rows, width = inputs.shape
    extra = 0 if tail is None else tail.shape[1]

    def kernel(inputs_ref, gain_ref, *refs):
        values = inputs_ref[...].astype(jnp.float32)
        meansq = jnp.mean(values * values, axis=-1, keepdims=True) + 1e-06
        refs[-1][:, :width] = (values * lax.rsqrt(meansq) * gain_ref[...]).astype(jnp.bfloat16)
        if extra:
            refs[-1][:, width:] = refs[0][...]

    shape = jax.ShapeDtypeStruct((rows, width + extra), jnp.bfloat16)
    operands = (inputs, gain) + (() if tail is None else (tail,))
    return call(kernel, shape, 4 * rows * width, 4 * rows * width)(*operands)


def hidden_of(tokens, gate_up):
    units = gate_up.shape[1] // 2
    both = jnp.dot(tokens, gate_up, preferred_element_type=jnp.float32)
    gated, upper = both[:, :units], both[:, units:]
    return gated / (1.0 + jnp.exp(-gated)) * upper


def hidden_rows(blocks, carriers, lanes, expert, gate_up):
    count = len(blocks)
    width, units = gate_up.shape[0], gate_up.shape[1] // 2
    rows = blocks[0].shape[0]
    given = []
    for block in list(blocks) + list(carriers):
        if not any(block is other for other in given):
            given.append(block)
    place = [[block is other for other in given].index(True) for block in blocks]
    bearer = [[block is other for other in given].index(True) for block in carriers]

    def kernel(expert_ref, gate_up_ref, *refs):
        mine = expert_ref[0].astype(jnp.float32)
        for i in range(count):
            hidden = hidden_of(refs[place[i]][:, :width], gate_up_ref[...])
            picks = refs[bearer[i]][:, lanes[i] : lanes[i] + 1].astype(jnp.float32)
            refs[len(given) + i][...] = jnp.where(picks == mine, hidden, 0.0).astype(
                jnp.bfloat16
            )

    shape = [jax.ShapeDtypeStruct((rows, units), jnp.bfloat16)] * count
    flops = 4 * count * rows * width * units
    vmem = pl.BlockSpec(memory_space=pltpu.VMEM)
    return call(
        kernel,
        shape,
        flops,
        4 * width * units + 2 * count * rows * width,
        in_specs=[pl.BlockSpec(memory_space=pltpu.SMEM)] + [vmem] * (1 + len(given)),
    )(expert, gate_up, *given)


def add_partial(hidden, down, arrived):
    def kernel(hidden_ref, down_ref, *refs):
        total = jnp.dot(hidden_ref[...], down_ref[...], preferred_element_type=jnp.float32)
        if arrived is not None:
            total = total + refs[0][...].astype(jnp.float32)
        refs[-1][...] = total.astype(jnp.bfloat16)

    rows, units = hidden.shape
    width = down.shape[1]
    shape = jax.ShapeDtypeStruct((rows, width), jnp.bfloat16)
    operands = (hidden, down) + (() if arrived is None else (arrived,))
    return call(kernel, shape, 2 * rows * units * width, 2 * units * width + 4 * rows * width)(
        *operands
    )


def finish(hidden, down, arrived, inputs, weights_in):
    def kernel(hidden_ref, down_ref, a_ref, b_ref, inputs_ref, weights_ref, out_ref):
        total = jnp.dot(hidden_ref[...], down_ref[...], preferred_element_type=jnp.float32)
        total = total + a_ref[...].astype(jnp.float32) + b_ref[...].astype(jnp.float32)
        moved = inputs_ref[...].astype(jnp.float32) + weights_ref[...] * total
        out_ref[...] = moved.astype(jnp.bfloat16)

    rows, width = inputs.shape
    shape = jax.ShapeDtypeStruct((rows, width), jnp.bfloat16)
    return call(kernel, shape, 2 * rows * hidden.shape[1] * width, 8 * rows * width)(
        hidden, down, *arrived, inputs, weights_in
    )


def per_device(
    inputs_down,
    inputs_up,
    routes_down,
    routes_up,
    probs_down,
    probs_up,
    norm_gain,
    gate_weight,
    up_weight,
    down_weight,
):
    down = down_weight[0]
    gate_up = jnp.concatenate([gate_weight[0], up_weight[0]], axis=1)
    acts_down, acts_up = inputs_down[0], inputs_up[0]
    rows, width = acts_down.shape
    ring = lax.axis_size("expert")
    half = ring // 2
    me = lax.axis_index("expert")
    my_expert = me // (ring // EXP_SECTION)
    forward = [(i, (i + 1) % ring) for i in range(ring)]
    backward = [(i, (i - 1) % ring) for i in range(ring)]

    expert = my_expert.astype(jnp.int32).reshape(1)

    picks = jnp.concatenate([routes_down[0], routes_up[0]], axis=1).astype(jnp.bfloat16)
    tail = jnp.repeat(picks, TAIL // 2, axis=1)
    lanes = (width, width + TAIL // 2)
    normed = (norm_rows(acts_down, norm_gain, tail), norm_rows(acts_up, norm_gain))

    hidden = [{}, {}]
    hidden[0][0], hidden[1][0] = hidden_rows(
        normed, (normed[0], normed[0]), lanes, expert, gate_up
    )
    ahead, behind = list(normed), list(normed)
    for step in range(1, half + 1):
        for way in range(2):
            if step < half or way == 0:
                ahead[way] = lax.ppermute(ahead[way], "expert", backward)
            if step < half or way == 1:
                behind[way] = lax.ppermute(behind[way], "expert", forward)
            if 1 < step < half:
                ahead[way], hidden[way][step - 1] = lax.optimization_barrier(
                    (ahead[way], hidden[way][step - 1])
                )
                behind[way], hidden[way][1 - step] = lax.optimization_barrier(
                    (behind[way], hidden[way][1 - step])
                )
        if step < half:
            (
                hidden[0][step],
                hidden[1][step],
                hidden[0][-step],
                hidden[1][-step],
            ) = hidden_rows(
                (ahead[0], ahead[1], behind[0], behind[1]),
                (ahead[0], ahead[0], behind[0], behind[0]),
                lanes * 2,
                expert,
                gate_up,
            )
        else:
            hidden[0][half], hidden[1][-half] = hidden_rows(
                (ahead[0], behind[1]), (ahead[0], ahead[0]), lanes, expert, gate_up
            )

    def add(way, offset, arrived):
        return add_partial(hidden[way][offset], down, arrived)

    onward, returning = [None, None], [None, None]
    for step in range(half, 0, -1):
        for way in range(2):
            if step < half or way == 0:
                onward[way] = lax.ppermute(add(way, step, onward[way]), "expert", forward)
            if step < half or way == 1:
                returning[way] = lax.ppermute(
                    add(way, -step, returning[way]), "expert", backward
                )
    moved_down, moved_up = (
        finish(hidden[way][0], down, (onward[way], returning[way]), acts, probs)
        for way, acts, probs in ((0, acts_down, probs_down[0]), (1, acts_up, probs_up[0]))
    )

    sections = lax.axis_size("section")
    next_down = lax.ppermute(
        moved_down, "section", [(i, (i + 1) % sections) for i in range(sections)]
    )
    next_up = lax.ppermute(
        moved_up, "section", [(i, (i - 1) % sections) for i in range(sections)]
    )
    return (next_down[None], next_up[None])


def solution(mesh):
    in_specs = (
        P("section", "expert", None),
        P("section", "expert", None),
        P("section", "expert", None),
        P("section", "expert", None),
        P("section", "expert", None),
        P("section", "expert", None),
        P("section", None),
        P("section", None, "expert"),
        P("section", None, "expert"),
        P("section", "expert", None),
    )
    out_specs = (P("section", "expert", None), P("section", "expert", None))
    return jax.shard_map(
        per_device, mesh=mesh, in_specs=in_specs, out_specs=out_specs, check_vma=False
    )
```

```python
import jax
import jax.numpy as jnp
from jax import lax
from jax.experimental import pallas as pl
from jax.experimental.pallas import tpu as pltpu
from jax.sharding import PartitionSpec as P

EXP_SECTION = 2
TAIL = 128
OWN_STEP = 1
BASE_STEPS = ((3, 4), (5, 6))
VMEM_LIMIT = 16 * 1024 * 1024


def call(kernel, out_shape, flops, moved, **options):
    return pl.pallas_call(
        kernel,
        out_shape=out_shape,
        cost_estimate=pl.CostEstimate(flops=flops, bytes_accessed=moved, transcendentals=0),
        compiler_params=pltpu.CompilerParams(vmem_limit_bytes=VMEM_LIMIT),
        **options,
    )


def norm_rows(inputs, gain, tail=None):
    rows, width = inputs.shape
    extra = 0 if tail is None else tail.shape[1]

    def kernel(inputs_ref, gain_ref, *refs):
        values = inputs_ref[...].astype(jnp.float32)
        meansq = jnp.mean(values * values, axis=-1, keepdims=True) + 1e-06
        refs[-1][:, :width] = (values * lax.rsqrt(meansq) * gain_ref[...]).astype(jnp.bfloat16)
        if extra:
            refs[-1][:, width:] = refs[0][...]

    shape = jax.ShapeDtypeStruct((rows, width + extra), jnp.bfloat16)
    operands = (inputs, gain) + (() if tail is None else (tail,))
    return call(kernel, shape, 4 * rows * width, 4 * rows * width)(*operands)


def hidden_of(tokens, gate, up):
    gated = jnp.dot(tokens, gate, preferred_element_type=jnp.float32)
    upper = jnp.dot(tokens, up, preferred_element_type=jnp.float32)
    return gated / (1.0 + jnp.exp(-gated)) * upper


def hidden_rows(blocks, carriers, lanes, expert, gate, up):
    count = len(blocks)
    width, units = gate.shape
    rows = blocks[0].shape[0]
    given = []
    for block in list(blocks) + list(carriers):
        if not any(block is other for other in given):
            given.append(block)
    place = [[block is other for other in given].index(True) for block in blocks]
    bearer = [[block is other for other in given].index(True) for block in carriers]

    def kernel(expert_ref, gate_ref, up_ref, *refs):
        mine = expert_ref[0].astype(jnp.float32)
        for i in range(count):
            hidden = hidden_of(refs[place[i]][:, :width], gate_ref[...], up_ref[...])
            picks = refs[bearer[i]][:, lanes[i] : lanes[i] + 1].astype(jnp.float32)
            refs[len(given) + i][...] = jnp.where(picks == mine, hidden, 0.0).astype(
                jnp.bfloat16
            )

    shape = [jax.ShapeDtypeStruct((rows, units), jnp.bfloat16)] * count
    flops = 4 * count * rows * width * units
    vmem = pl.BlockSpec(memory_space=pltpu.VMEM)
    return call(
        kernel,
        shape,
        flops,
        4 * width * units + 2 * count * rows * width,
        in_specs=[pl.BlockSpec(memory_space=pltpu.SMEM)] + [vmem] * (2 + len(given)),
    )(expert, gate, up, *given)


def add_partial(hidden, down, arrived):
    def kernel(hidden_ref, down_ref, *refs):
        total = jnp.dot(hidden_ref[...], down_ref[...], preferred_element_type=jnp.float32)
        if arrived is not None:
            total = total + refs[0][...].astype(jnp.float32)
        refs[-1][...] = total.astype(jnp.bfloat16)

    rows, units = hidden.shape
    width = down.shape[1]
    shape = jax.ShapeDtypeStruct((rows, width), jnp.bfloat16)
    operands = (hidden, down) + (() if arrived is None else (arrived,))
    return call(kernel, shape, 2 * rows * units * width, 2 * units * width + 4 * rows * width)(
        *operands
    )


def residual(hidden, down, inputs, weights_in):
    rows, width = inputs.shape

    def kernel(hidden_ref, down_ref, inputs_ref, weights_ref, high_ref, low_ref):
        own = jnp.dot(hidden_ref[...], down_ref[...], preferred_element_type=jnp.float32)
        total = inputs_ref[...].astype(jnp.float32) + weights_ref[...] * own
        high = total.astype(jnp.bfloat16)
        high_ref[:, :width] = high
        low_ref[...] = (total - high.astype(jnp.float32)).astype(jnp.bfloat16)
        lane = lax.broadcasted_iota(jnp.int32, (rows, TAIL), 1)
        rest = jnp.broadcast_to(weights_ref[...], (rows, TAIL))
        columns = jnp.zeros((rows, TAIL), jnp.float32)
        for part in range(3):
            piece = rest.astype(jnp.bfloat16).astype(jnp.float32)
            columns = jnp.where(lane == part, piece, columns)
            rest = rest - piece
        high_ref[:, width:] = columns.astype(jnp.bfloat16)

    shape = [
        jax.ShapeDtypeStruct((rows, width + TAIL), jnp.bfloat16),
        jax.ShapeDtypeStruct((rows, width), jnp.bfloat16),
    ]
    return call(kernel, shape, 2 * rows * hidden.shape[1] * width, 8 * rows * width)(
        hidden, down, inputs, weights_in
    )


def finish(base, arrived):
    high, low = base
    rows, width = low.shape

    def kernel(high_ref, low_ref, a_ref, b_ref, out_ref):
        weight = jnp.sum(
            high_ref[:, width:].astype(jnp.float32), axis=1, keepdims=True
        )
        total = a_ref[...].astype(jnp.float32) + b_ref[...].astype(jnp.float32)
        moved = high_ref[:, :width].astype(jnp.float32) + low_ref[...].astype(jnp.float32)
        out_ref[0] = (moved + weight * total).astype(jnp.bfloat16)

    shape = jax.ShapeDtypeStruct((1, rows, width), jnp.bfloat16)
    return call(kernel, shape, 4 * rows * width, 10 * rows * width)(high, low, *arrived)


def per_device(
    inputs_down,
    inputs_up,
    routes_down,
    routes_up,
    probs_down,
    probs_up,
    norm_gain,
    gate_weight,
    up_weight,
    down_weight,
):
    gate, up, down = gate_weight[0], up_weight[0], down_weight[0]
    acts_down, acts_up = inputs_down[0], inputs_up[0]
    rows, width = acts_down.shape
    ring = lax.axis_size("expert")
    half = ring // 2
    me = lax.axis_index("expert")
    my_expert = me // (ring // EXP_SECTION)
    forward = [(i, (i + 1) % ring) for i in range(ring)]
    backward = [(i, (i - 1) % ring) for i in range(ring)]

    expert = my_expert.astype(jnp.int32).reshape(1)

    picks = jnp.concatenate([routes_down[0], routes_up[0]], axis=1).astype(jnp.bfloat16)
    tail = jnp.repeat(picks, TAIL // 2, axis=1)
    lanes = (width, width + TAIL // 2)
    normed = (norm_rows(acts_down, norm_gain, tail), norm_rows(acts_up, norm_gain))

    hidden = [{}, {}]
    ahead, behind = list(normed), list(normed)
    for step in range(1, half + 1):
        for way in range(2):
            if step < half or way == 0:
                ahead[way] = lax.ppermute(ahead[way], "expert", backward)
            if step < half or way == 1:
                behind[way] = lax.ppermute(behind[way], "expert", forward)
            if 1 < step < half:
                ahead[way], hidden[way][step - 1] = lax.optimization_barrier(
                    (ahead[way], hidden[way][step - 1])
                )
                behind[way], hidden[way][1 - step] = lax.optimization_barrier(
                    (behind[way], hidden[way][1 - step])
                )
            if step in BASE_STEPS[way]:
                part = BASE_STEPS[way].index(step)
                ahead[way], base[way][part] = lax.optimization_barrier(
                    (ahead[way], base[way][part])
                )
        if step == OWN_STEP:
            behind[0], *mine = lax.optimization_barrier((behind[0], *normed))
            hidden[0][0], hidden[1][0] = hidden_rows(
                mine, (mine[0], mine[0]), lanes, expert, gate, up
            )
            sections = lax.axis_size("section")
            base = [None, None]
            for way, acts, probs in ((0, acts_down, probs_down[0]), (1, acts_up, probs_up[0])):
                route = [(i, (i + 1 - 2 * way) % sections) for i in range(sections)]
                base[way] = [
                    lax.ppermute(part, "section", route)
                    for part in residual(hidden[way][0], down, acts, probs)
                ]
        if step < half:
            (
                hidden[0][step],
                hidden[1][step],
                hidden[0][-step],
                hidden[1][-step],
            ) = hidden_rows(
                (ahead[0], ahead[1], behind[0], behind[1]),
                (ahead[0], ahead[0], behind[0], behind[0]),
                lanes * 2,
                expert,
                gate,
                up,
            )
        else:
            hidden[0][half], hidden[1][-half] = hidden_rows(
                (ahead[0], behind[1]), (ahead[0], ahead[0]), lanes, expert, gate, up
            )

    def add(way, offset, arrived):
        return add_partial(hidden[way][offset], down, arrived)

    def last_hop(value, way, shift):
        route = [
            (i * ring + j, (i + 1 - 2 * way) % sections * ring + (j + shift) % ring)
            for i in range(sections)
            for j in range(ring)
        ]
        return lax.ppermute(value, ("section", "expert"), route)

    onward, returning = [None, None], [None, None]
    for step in range(half, 0, -1):
        for way in range(2):
            if step < half or way == 0:
                onward[way] = add(way, step, onward[way])
                if step > 1:
                    onward[way] = lax.ppermute(onward[way], "expert", forward)
                else:
                    onward[way] = last_hop(onward[way], way, 1)
            if step < half or way == 1:
                returning[way] = add(way, -step, returning[way])
                if step > 1:
                    returning[way] = lax.ppermute(returning[way], "expert", backward)
                else:
                    returning[way] = last_hop(returning[way], way, -1)
    return tuple(finish(base[way], (onward[way], returning[way])) for way in range(2))


def solution(mesh):
    in_specs = (
        P("section", "expert", None),
        P("section", "expert", None),
        P("section", "expert", None),
        P("section", "expert", None),
        P("section", "expert", None),
        P("section", "expert", None),
        P("section", None),
        P("section", None, "expert"),
        P("section", None, "expert"),
        P("section", "expert", None),
    )
    out_specs = (P("section", "expert", None), P("section", "expert", None))
    return jax.shard_map(
        per_device, mesh=mesh, in_specs=in_specs, out_specs=out_specs, check_vma=False
    )
```

```python
import jax
import jax.numpy as jnp
from jax import lax
from jax.experimental import pallas as pl
from jax.experimental.pallas import tpu as pltpu
from jax.sharding import PartitionSpec as P

EXP_SECTION = 2
TAIL = 128
OWN_STEP = 1
BASE_STEPS = ((4, 5), (6, 7))
VMEM_LIMIT = 16 * 1024 * 1024


def call(kernel, out_shape, flops, moved, **options):
    return pl.pallas_call(
        kernel,
        out_shape=out_shape,
        cost_estimate=pl.CostEstimate(flops=flops, bytes_accessed=moved, transcendentals=0),
        compiler_params=pltpu.CompilerParams(vmem_limit_bytes=VMEM_LIMIT),
        **options,
    )


def norm_of(inputs, gain):
    values = inputs.astype(jnp.float32)
    meansq = jnp.mean(values * values, axis=-1, keepdims=True) + 1e-06
    return (values * lax.rsqrt(meansq) * gain).astype(jnp.bfloat16)


def norm_rows(inputs, gain, picks, other_picks):
    rows, width = inputs.shape

    def kernel(inputs_ref, gain_ref, picks_ref, other_ref, out_ref):
        out_ref[:, :width] = norm_of(inputs_ref[...], gain_ref[...])
        lane = lax.broadcasted_iota(jnp.int32, (rows, TAIL), 1)
        routes = jnp.where(lane < TAIL // 2, picks_ref[...], other_ref[...])
        out_ref[:, width:] = routes.astype(jnp.float32).astype(jnp.bfloat16)

    shape = jax.ShapeDtypeStruct((rows, width + TAIL), jnp.bfloat16)
    return call(kernel, shape, 50000 * rows * width, 4 * rows * width)(
        inputs, gain, picks, other_picks
    )


def hidden_of(tokens, gate, up):
    gated = jnp.dot(tokens, gate, preferred_element_type=jnp.float32)
    upper = jnp.dot(tokens, up, preferred_element_type=jnp.float32)
    return gated / (1.0 + jnp.exp(-gated)) * upper


def hidden_rows(blocks, carriers, lanes, expert, gain, gate, up):
    count = len(blocks)
    width, units = gate.shape
    rows = blocks[0].shape[0]
    given = []
    for block in list(blocks) + list(carriers):
        if not any(block is other for other in given):
            given.append(block)
    place = [[block is other for other in given].index(True) for block in blocks]
    bearer = [[block is other for other in given].index(True) for block in carriers]

    def kernel(expert_ref, gain_ref, gate_ref, up_ref, *refs):
        mine = expert_ref[0].astype(jnp.float32)
        for i in range(count):
            tokens = refs[place[i]][:, :width]
            if blocks[i].shape[1] == width:
                tokens = norm_of(tokens, gain_ref[...])
            hidden = hidden_of(tokens, gate_ref[...], up_ref[...])
            picks = refs[bearer[i]][:, lanes[i] : lanes[i] + 1].astype(jnp.float32)
            refs[len(given) + i][...] = jnp.where(picks == mine, hidden, 0.0).astype(
                jnp.bfloat16
            )

    shape = [jax.ShapeDtypeStruct((rows, units), jnp.bfloat16)] * count
    flops = 4 * count * rows * width * units
    vmem = pl.BlockSpec(memory_space=pltpu.VMEM)
    return call(
        kernel,
        shape,
        flops,
        4 * width * units + 2 * count * rows * width,
        in_specs=[pl.BlockSpec(memory_space=pltpu.SMEM)] + [vmem] * (3 + len(given)),
    )(expert, gain, gate, up, *given)


def add_partial(hidden, down, arrived):
    def kernel(hidden_ref, down_ref, *refs):
        total = jnp.dot(hidden_ref[...], down_ref[...], preferred_element_type=jnp.float32)
        if arrived is not None:
            total = total + refs[0][...].astype(jnp.float32)
        refs[-1][...] = total.astype(jnp.bfloat16)

    rows, units = hidden.shape
    width = down.shape[1]
    shape = jax.ShapeDtypeStruct((rows, width), jnp.bfloat16)
    operands = (hidden, down) + (() if arrived is None else (arrived,))
    return call(kernel, shape, 2 * rows * units * width, 2 * units * width + 4 * rows * width)(
        *operands
    )


def residual(hidden, down, inputs, weights_in):
    rows, width = inputs.shape

    def kernel(hidden_ref, down_ref, inputs_ref, weights_ref, high_ref, low_ref):
        own = jnp.dot(hidden_ref[...], down_ref[...], preferred_element_type=jnp.float32)
        total = inputs_ref[...].astype(jnp.float32) + weights_ref[...] * own
        high = total.astype(jnp.bfloat16)
        high_ref[:, :width] = high
        low_ref[...] = (total - high.astype(jnp.float32)).astype(jnp.bfloat16)
        lane = lax.broadcasted_iota(jnp.int32, (rows, TAIL), 1)
        rest = jnp.broadcast_to(weights_ref[...], (rows, TAIL))
        columns = jnp.zeros((rows, TAIL), jnp.float32)
        for part in range(3):
            piece = rest.astype(jnp.bfloat16).astype(jnp.float32)
            columns = jnp.where(lane == part, piece, columns)
            rest = rest - piece
        high_ref[:, width:] = columns.astype(jnp.bfloat16)

    shape = [
        jax.ShapeDtypeStruct((rows, width + TAIL), jnp.bfloat16),
        jax.ShapeDtypeStruct((rows, width), jnp.bfloat16),
    ]
    return call(kernel, shape, 2 * rows * hidden.shape[1] * width, 8 * rows * width)(
        hidden, down, inputs, weights_in
    )


def finish(bases, sums):
    rows, width = bases[0][1].shape

    def kernel(*refs):
        for way in range(2):
            high_ref, low_ref, a_ref, b_ref = refs[4 * way : 4 * way + 4]
            weight = jnp.sum(high_ref[:, width:].astype(jnp.float32), axis=1, keepdims=True)
            total = a_ref[...].astype(jnp.float32) + b_ref[...].astype(jnp.float32)
            moved = high_ref[:, :width].astype(jnp.float32) + low_ref[...].astype(jnp.float32)
            refs[8 + way][0] = (moved + weight * total).astype(jnp.bfloat16)

    shape = [jax.ShapeDtypeStruct((1, rows, width), jnp.bfloat16)] * 2
    operands = [value for way in range(2) for value in (*bases[way], *sums[way])]
    return call(kernel, shape, 8 * rows * width, 20 * rows * width)(*operands)


def per_device(
    inputs_down,
    inputs_up,
    routes_down,
    routes_up,
    probs_down,
    probs_up,
    norm_gain,
    gate_weight,
    up_weight,
    down_weight,
):
    gate, up, down = gate_weight[0], up_weight[0], down_weight[0]
    acts_down, acts_up = inputs_down[0], inputs_up[0]
    rows, width = acts_down.shape
    ring = lax.axis_size("expert")
    half = ring // 2
    me = lax.axis_index("expert")
    my_expert = me // (ring // EXP_SECTION)
    plus = [(i, (i + 1) % ring) for i in range(ring)]
    minus = [(i, (i - 1) % ring) for i in range(ring)]

    expert = my_expert.astype(jnp.int32).reshape(1)

    lanes = (width, width + TAIL // 2)
    sent = (norm_rows(acts_down, norm_gain, routes_down[0], routes_up[0]), acts_up)

    hidden = [{}, {}]
    ahead, behind = list(sent), list(sent)
    for step in range(1, half + 1):
        for way in (1, 0):
            if step < half or way == 0:
                ahead[way] = lax.ppermute(ahead[way], "expert", plus)
            if step < half or way == 1:
                behind[way] = lax.ppermute(behind[way], "expert", minus)
            if 1 < step < half:
                ahead[way], hidden[way][step - 1] = lax.optimization_barrier(
                    (ahead[way], hidden[way][step - 1])
                )
                behind[way], hidden[way][1 - step] = lax.optimization_barrier(
                    (behind[way], hidden[way][1 - step])
                )
            if step in BASE_STEPS[way]:
                part = BASE_STEPS[way].index(step)
                ahead[way], base[way][part] = lax.optimization_barrier(
                    (ahead[way], base[way][part])
                )
        if step == OWN_STEP:
            behind[0], *mine = lax.optimization_barrier((behind[0], *sent))
            hidden[0][0], hidden[1][0] = hidden_rows(
                mine, (mine[0], mine[0]), lanes, expert, norm_gain, gate, up
            )
            sections = lax.axis_size("section")
            base = [None, None]
            for way, acts, probs in ((0, acts_down, probs_down[0]), (1, acts_up, probs_up[0])):
                route = [(i, (i + 1 - 2 * way) % sections) for i in range(sections)]
                base[way] = [
                    lax.ppermute(part, "section", route)
                    for part in residual(hidden[way][0], down, acts, probs)
                ]
        if step < half:
            (
                hidden[0][step],
                hidden[1][step],
                hidden[0][-step],
                hidden[1][-step],
            ) = hidden_rows(
                (ahead[0], ahead[1], behind[0], behind[1]),
                (ahead[0], ahead[0], behind[0], behind[0]),
                lanes * 2,
                expert,
                norm_gain,
                gate,
                up,
            )
        else:
            hidden[0][half], hidden[1][-half] = hidden_rows(
                (ahead[0], behind[1]), (ahead[0], ahead[0]), lanes, expert, norm_gain, gate, up
            )

    def add(way, offset, arrived):
        return add_partial(hidden[way][offset], down, arrived)

    def last_hop(value, way, shift):
        route = [
            (i * ring + j, (i + 1 - 2 * way) % sections * ring + (j + shift) % ring)
            for i in range(sections)
            for j in range(ring)
        ]
        return lax.ppermute(value, ("section", "expert"), route)

    onward, returning = [None, None], [None, None]
    for step in range(half, 0, -1):
        for way in range(2):
            if step < half or way == 0:
                onward[way] = add(way, step, onward[way])
                if step > 1:
                    onward[way] = lax.ppermute(onward[way], "expert", minus)
                else:
                    onward[way] = last_hop(onward[way], way, -1)
            if step < half or way == 1:
                returning[way] = add(way, -step, returning[way])
                if step > 1:
                    returning[way] = lax.ppermute(returning[way], "expert", plus)
                else:
                    returning[way] = last_hop(returning[way], way, 1)
    return tuple(finish(base, list(zip(onward, returning))))


def solution(mesh):
    in_specs = (
        P("section", "expert", None),
        P("section", "expert", None),
        P("section", "expert", None),
        P("section", "expert", None),
        P("section", "expert", None),
        P("section", "expert", None),
        P("section", None),
        P("section", None, "expert"),
        P("section", None, "expert"),
        P("section", "expert", None),
    )
    out_specs = (P("section", "expert", None), P("section", "expert", None))
    return jax.shard_map(
        per_device, mesh=mesh, in_specs=in_specs, out_specs=out_specs, check_vma=False
    )
```
